768 devices in a mesh: row: 64 (over y, x, core), col: 12 (over z).
Axes of the slice: x: 4, y: 8, z: 12, core: 2. Of those that a mesh axis runs over, the one named last changes fastest.
Arguments:
- features: bfloat16 [98304, 128], P(('row', 'col')), may hold values from -6 to 6
- node_order: int32 [768, 128], P(('row', 'col')), may hold values from 0 to 127, each once within a row
- adj_tiles: bfloat16 [768, 32, 128, 128], P(('row', 'col')), may hold values from 0 to 0.026977539
- tile_rows: int32 [768, 32], P(('row', 'col')), may hold values from 0 to 63
- tile_cols: int32 [768, 32], P(('row', 'col')), may hold values from 0 to 11
- w_self: bfloat16 [128, 256], replicated, may hold values from -0.5 to 0.5
- w_neigh: bfloat16 [128, 256], replicated, may hold values from -0.5 to 0.5
- bias_vector: float32 [256], replicated, may hold values from -3 to 3
- cotangent: bfloat16 [98304, 256], P(('row', 'col')), may hold values from -6 to 6
Outputs:
- hidden_out: bfloat16 [98304, 256], P(('row', 'col'))
- feature_grad: float32 [98304, 128], P(('row', 'col'))
The draws below stay inside these ranges and needn't reach their ends.
Inputs may be any that keep to these rules, and one draw needn't show every extreme that they name: `node_order`: each row is a permutation of 0 .. 127.
All inputs are finite; a program needn't handle non-finite values.
Results may differ from the reference program's by a relative error of at most 0.015.
Values may be sent and summed in bfloat16 or wider, within the bound.
No kernel may reach another device: no remote copies, remote signals or barrier semaphores. Data moves between devices by JAX's collectives and lax.ppermute only.
A program may use at most 32 MiB of HBM per device.

```python
import math
import jax
import jax.numpy as jnp
import numpy as np
from jax import lax

BLOCK = 128
FEAT = 128
HIDDEN_SIZE = 256
TILES = 32
ROWGROUP = 64
COLGROUP = 12
NODES = 98304


def touch_ends(result, key, low, high):
    spot = [jax.random.randint(jax.random.fold_in(key, axis), (), 0, length) for axis, length in enumerate(result.shape)]
    widest = result.shape.index(max(result.shape))
    neighbour = spot[:widest] + [(spot[widest] + 1) % result.shape[widest]] + spot[widest + 1:]
    return result.at[tuple(spot)].set(low).at[tuple(neighbour)].set(high)


def block_levels(key, dims, cuts, least, top_value):
    factor_of = 1.0
    for axis_at, parts in cuts:
        draws = jax.random.uniform(jax.random.fold_in(jax.random.fold_in(key, 6), axis_at), (parts,), jnp.float32, least / len(cuts), top_value / len(cuts))
        factor_of = factor_of * jnp.repeat(jnp.exp(draws), dims[axis_at] // parts).reshape((-1,) + (1,) * (len(dims) - 1 - axis_at))
    return factor_of


def rank_table(count, slope):
    weights = [(1 << 20) // math.isqrt(rank ** slope) + 1 for rank in range(1, count + 1)]
    scale = 1 + sum(weights) // (1 << 30)
    return np.cumsum(np.array([max(1, weight // scale) for weight in weights]))


def ranked_ids(stream_key, extent, number_of, lean):
    grid = rank_table(number_of, lean)
    lot = jax.random.randint(jax.random.fold_in(stream_key, 1), extent, 0, int(grid[number_of - 1]))
    rank = jnp.searchsorted(jnp.asarray(grid, jnp.int32), lot, side="right")
    return jax.random.permutation(jax.random.fold_in(stream_key, 2), number_of)[rank].astype(jnp.int32)


def gaussian(key, dims, deviation, bound, pieces=(), kind=jnp.bfloat16):
    result = deviation * jax.random.normal(key, dims, jnp.float32)
    if pieces:
        result = result * block_levels(key, dims, pieces, -0.22, 0.18)
    return jnp.clip(result, -bound, bound).astype(kind)


def setup_inputs(seed: int = 0) -> dict:
    key_list = jax.random.split(jax.random.key(seed), 10)
    return {
        "features": gaussian(key_list[0], (NODES, FEAT), 1.0, 6.0, ((0, 768),)),
        "node_order": jax.vmap(lambda own: jax.random.permutation(own, BLOCK))(jax.random.split(key_list[1], (ROWGROUP * COLGROUP))).reshape((ROWGROUP * COLGROUP, BLOCK)).astype(jnp.int32),
        "adj_tiles": jnp.clip(0.026977539 * jax.random.uniform(key_list[2], (ROWGROUP * COLGROUP, TILES, BLOCK, BLOCK), jnp.float32) ** block_levels(key_list[2], (ROWGROUP * COLGROUP, TILES, BLOCK, BLOCK), ((0, 768),), -0.2, 0.2), 0.0, 0.026977539).astype(jnp.bfloat16),
        "tile_rows": touch_ends(ranked_ids(key_list[3], (ROWGROUP * COLGROUP, TILES), ROWGROUP, 2), jax.random.fold_in(key_list[3], 3), 0, ROWGROUP - 1).astype(jnp.int32),
        "tile_cols": touch_ends(jax.random.randint(key_list[4], (ROWGROUP * COLGROUP, TILES), 0, COLGROUP), jax.random.fold_in(key_list[4], 1), 0, COLGROUP - 1).astype(jnp.int32),
        "w_self": gaussian(key_list[5], (FEAT, HIDDEN_SIZE), FEAT ** -0.5, 0.5),
        "w_neigh": gaussian(key_list[6], (FEAT, HIDDEN_SIZE), FEAT ** -0.5, 0.5),
        "bias_vector": gaussian(key_list[7], (HIDDEN_SIZE,), 0.5, 3.0, (), jnp.float32),
        "cotangent": gaussian(key_list[8], (NODES, HIDDEN_SIZE), 1.0, 6.0, ((0, 768),)),
    }


def reference(features, node_order, adj_tiles, tile_rows, tile_cols, w_self, w_neigh, bias_vector, cotangent):
    node_count = features.shape[0]
    block_count = node_count // BLOCK
    block_base = (jnp.arange(block_count, dtype=jnp.int32) * BLOCK)[:, None]
    node_index = (block_base + node_order.astype(jnp.int32)).reshape(-1)
    blocked = features[node_index]
    source_blocks = blocked.reshape(block_count, BLOCK, FEAT)
    device_ids = jnp.arange(block_count, dtype=jnp.int32)

    def forward_step(running, scan_item):
        device, tile_block, target, source = scan_item
        row_pos = device // COLGROUP
        col_pos = device % COLGROUP
        picked = source_blocks[row_pos * COLGROUP + source].astype(jnp.float32)
        products = jnp.einsum("kij,kjf->kif", tile_block.astype(jnp.float32), picked)
        return running.at[target * COLGROUP + col_pos].add(products), None

    empty_sum = jnp.zeros((block_count, BLOCK, FEAT), jnp.float32)
    summed, _ = lax.scan(forward_step, empty_sum, (device_ids, adj_tiles, tile_rows, tile_cols))
    aggregated = summed.reshape(node_count, FEAT).astype(jnp.bfloat16)
    pre_activation = (jnp.dot(blocked, w_self, preferred_element_type=jnp.float32)
                      + jnp.dot(aggregated, w_neigh, preferred_element_type=jnp.float32)
                      + bias_vector.astype(jnp.float32))
    squash = jax.nn.sigmoid(pre_activation)
    hidden_rows = (pre_activation * squash).astype(jnp.bfloat16)
    hidden_out = jnp.zeros((node_count, HIDDEN_SIZE), jnp.bfloat16).at[node_index].set(hidden_rows)
    grad_rows = cotangent[node_index].astype(jnp.float32)
    grad_pre = (grad_rows * squash * (1.0 + pre_activation * (1.0 - squash))).astype(jnp.bfloat16)
    grad_agg = jnp.dot(grad_pre, w_neigh.T, preferred_element_type=jnp.float32).astype(jnp.bfloat16)
    agg_blocks = grad_agg.reshape(block_count, BLOCK, FEAT)

    def backward_step(running, scan_item):
        device, tile_block, target, source = scan_item
        row_pos = device // COLGROUP
        col_pos = device % COLGROUP
        gathered = agg_blocks[target * COLGROUP + col_pos].astype(jnp.float32)
        back_terms = jnp.einsum("kij,kif->kjf", tile_block.astype(jnp.float32), gathered)
        return running.at[row_pos * COLGROUP + source].add(back_terms), None

    spread, _ = lax.scan(backward_step, empty_sum, (device_ids, adj_tiles, tile_rows, tile_cols))
    grad_blocked = jnp.dot(grad_pre, w_self.T, preferred_element_type=jnp.float32) + spread.reshape(node_count, FEAT)
    feature_grad = jnp.zeros((node_count, FEAT), jnp.float32).at[node_index].set(grad_blocked)
    return hidden_out, feature_grad
```

```python
import jax
import jax.numpy as jnp
from jax import lax
from jax.experimental import pallas as pl
from jax.experimental.pallas import tpu as pltpu
from jax.sharding import PartitionSpec as P

BF16 = jnp.bfloat16
F32 = jnp.float32
VMEM = pl.BlockSpec(memory_space=pltpu.VMEM)
SMEM = pl.BlockSpec(memory_space=pltpu.SMEM)


def matmul(a, b):
    return lax.dot_general(a, b, (((1,), (0,)), ((), ())), preferred_element_type=F32)


def matmul_nt(a, b):
    return lax.dot_general(a, b, (((1,), (1,)), ((), ())), preferred_element_type=F32)


def matmul_tn(a, b):
    return lax.dot_general(a, b, (((0,), (0,)), ((), ())), preferred_element_type=F32)


def place_matrix(order_ref):
    order = order_ref[...]
    size = order.shape[1]
    nodes = lax.broadcasted_iota(jnp.int32, (size, size), 0)
    return jnp.where(nodes == order, 1.0, 0.0).astype(BF16)


def order_kernel(order_ref, features_ref, blocked_ref):
    place = place_matrix(order_ref)
    blocked_ref[...] = matmul_tn(place, features_ref[...]).astype(BF16)


def forward_kernel(rows_ref, cols_ref, tiles_ref, sources_ref, keep_ref, send_ref, total):
    core = lax.rem(lax.axis_index("row"), 2)
    total[...] = jnp.zeros_like(total)
    for k in range(tiles_ref.shape[1]):
        target = rows_ref[0, k]
        product = matmul(tiles_ref[0, k], sources_ref[cols_ref[0, k]])
        away = lax.rem(target + core, 2)
        total[away, target // 2] += product
    keep_ref[...] = total[0]
    send_ref[...] = total[1].astype(BF16)


def middle_kernel(
    parts_ref,
    blocked_ref,
    order_ref,
    w_self_ref,
    w_neigh_ref,
    bias_ref,
    cotangent_ref,
    hidden_ref,
    spread_ref,
    self_grad_ref,
):
    place = place_matrix(order_ref)
    aggregated = jnp.sum(parts_ref[...].astype(F32), axis=0).astype(BF16)
    pre_activation = (
        matmul(blocked_ref[...], w_self_ref[...])
        + matmul(aggregated, w_neigh_ref[...])
        + bias_ref[...]
    )
    squash = jax.nn.sigmoid(pre_activation)
    hidden_rows = (pre_activation * squash).astype(BF16)
    hidden_ref[...] = matmul(place, hidden_rows).astype(BF16)
    grad_rows = matmul_tn(place, cotangent_ref[...])
    grad_pre = (grad_rows * squash * (1.0 + pre_activation * (1.0 - squash))).astype(BF16)
    grad_agg = matmul_nt(w_neigh_ref[...], grad_pre).astype(BF16)
    spread_ref[...] = jnp.broadcast_to(grad_agg[None], spread_ref.shape)
    self_grad_ref[...] = matmul_nt(w_self_ref[...], grad_pre)


def backward_kernel(rows_ref, cols_ref, tiles_ref, near_ref, far_ref, parts_ref, total):
    core = lax.rem(lax.axis_index("row"), 2)
    total[...] = jnp.zeros_like(total)
    for k in range(tiles_ref.shape[1]):
        target = rows_ref[0, k]
        away = lax.rem(target + core, 2)
        grads = jnp.where(away == 0, near_ref[target // 2], far_ref[target // 2])
        total[cols_ref[0, k]] += matmul(grads, tiles_ref[0, k])
    parts_ref[...] = total[...].astype(BF16)


def last_kernel(parts_ref, self_grad_ref, order_ref, out_ref):
    place = place_matrix(order_ref)
    grads = self_grad_ref[...] + jnp.sum(parts_ref[...].astype(F32), axis=0)
    high = grads.astype(BF16)
    rest = grads - high.astype(F32)
    middle = rest.astype(BF16)
    low = (rest - middle.astype(F32)).astype(BF16)
    out_ref[...] = matmul_nt(place, high) + (matmul_nt(place, middle) + matmul_nt(place, low))


def call(kernel, outs, specs, scratch=(), flops=0):
    moved = sum(o.size * o.dtype.itemsize for o in outs)
    return pl.pallas_call(
        kernel,
        out_shape=outs,
        in_specs=specs,
        out_specs=[VMEM] * len(outs),
        scratch_shapes=list(scratch),
        compiler_params=pltpu.CompilerParams(vmem_limit_bytes=24 * 1024 * 1024),
        cost_estimate=pl.CostEstimate(flops=flops, bytes_accessed=moved, transcendentals=0),
    )


def per_device(
    features, node_order, adj_tiles, tile_rows, tile_cols, w_self, w_neigh, bias_vector, cotangent
):
    block, feat = features.shape
    hidden = w_self.shape[1]
    row_count = lax.axis_size("row")
    col_count = lax.axis_size("col")
    tiles = adj_tiles.shape[1]
    chips = row_count // 2
    planes = [[2 * chip + core for chip in range(chips)] for core in range(2)]
    partners = [(i, i ^ 1) for i in range(row_count)]
    shape = jax.ShapeDtypeStruct
    tile_flops = 2 * tiles * block * block * feat

    (blocked,) = call(order_kernel, [shape((block, feat), BF16)], [VMEM] * 2)(node_order, features)
    sources = lax.all_gather(blocked, "col", axis=0)
    keep, send = call(
        forward_kernel,
        [shape((chips, block, feat), F32), shape((chips, block, feat), BF16)],
        [SMEM, SMEM, VMEM, VMEM],
        [pltpu.VMEM((2, chips, block, feat), F32)],
        tile_flops,
    )(tile_rows, tile_cols, adj_tiles, sources)
    other = lax.ppermute(send, "row", partners)
    chip_sum = (keep + other.astype(F32)).astype(BF16)
    parts = lax.all_to_all(chip_sum, "row", 0, 0, axis_index_groups=planes)
    hidden_out, spread, self_grad = call(
        middle_kernel,
        [
            shape((block, hidden), BF16),
            shape((chips, feat, block), BF16),
            shape((feat, block), F32),
        ],
        [VMEM] * 7,
    )(parts, blocked, node_order, w_self, w_neigh, bias_vector.reshape(1, hidden), cotangent)
    near = lax.all_to_all(spread, "row", 0, 0, axis_index_groups=planes)
    far = lax.ppermute(near, "row", partners)
    (source_parts,) = call(
        backward_kernel,
        [shape((col_count, feat, block), BF16)],
        [SMEM, SMEM, VMEM, VMEM, VMEM],
        [pltpu.VMEM((col_count, feat, block), F32)],
        tile_flops,
    )(tile_rows, tile_cols, adj_tiles, near, far)
    own_parts = lax.all_to_all(source_parts, "col", 0, 0)
    (feature_grad,) = call(last_kernel, [shape((block, feat), F32)], [VMEM] * 3)(
        own_parts, self_grad, node_order
    )
    return (hidden_out, feature_grad)


def solution(mesh):
    placed = (
        P(("row", "col"), None),
        P(("row", "col"), None),
        P(("row", "col"), None, None, None),
        P(("row", "col"), None),
        P(("row", "col"), None),
        P(),
        P(),
        P(),
        P(("row", "col"), None),
    )
    return jax.shard_map(
        per_device,
        mesh=mesh,
        in_specs=placed,
        out_specs=(P(("row", "col"), None), P(("row", "col"), None)),
        check_vma=False,
    )
```

```python
import jax
import jax.numpy as jnp
from jax import lax
from jax.experimental import pallas as pl
from jax.experimental.pallas import tpu as pltpu
from jax.sharding import PartitionSpec as P

BF16 = jnp.bfloat16
F32 = jnp.float32
WIDTH = 4
ANY = pl.BlockSpec(memory_space=pl.ANY)
VMEM = pl.BlockSpec(memory_space=pltpu.VMEM)
SMEM = pl.BlockSpec(memory_space=pltpu.SMEM)


def matmul(a, b):
    return lax.dot_general(a, b, (((1,), (0,)), ((), ())), preferred_element_type=F32)


def matmul_nt(a, b):
    return lax.dot_general(a, b, (((1,), (1,)), ((), ())), preferred_element_type=F32)


def matmul_tn(a, b):
    return lax.dot_general(a, b, (((0,), (0,)), ((), ())), preferred_element_type=F32)


def column_pairs(rows, cols, turned):
    groups = []
    for row in range(rows):
        shift = 1 if row % 2 in turned else 0
        for col in range(shift, cols + shift, 2):
            pair = sorted([col, (col + 1) % cols], key=lambda v: v % 2)
            groups.append([row * cols + c for c in pair])
    return groups


def column_halves(rows, cols):
    return [
        [row * cols + c for c in range(odd, cols, 2)] for row in range(rows) for odd in range(2)
    ]


def place_matrix(order_ref):
    order = order_ref[...]
    size = order.shape[1]
    nodes = lax.broadcasted_iota(jnp.int32, (size, size), 0)
    return jnp.where(nodes == order, 1.0, 0.0).astype(BF16)


def seat(target):
    core = target & 1
    kind = ((target >> 3) & 1) * 2 + ((target >> 1) & 1)
    place = (target >> 4) * 2 + ((target >> 2) & 1)
    return core, kind, place


def near_groups(chips, turned):
    height = chips // WIDTH
    groups = []
    for core in range(2):
        shift = 1 if core in turned else 0
        for y in range(shift, height + shift, 2):
            for x in range(shift, WIDTH + shift, 2):
                ys = sorted([y, (y + 1) % height], key=lambda v: v % 2)
                xs = sorted([x, (x + 1) % WIDTH], key=lambda v: v % 2)
                groups.append([(b * WIDTH + a) * 2 + core for b in ys for a in xs])
    return groups


def far_groups(chips):
    height = chips // WIDTH
    return [
        [(y * WIDTH + x) * 2 + core for y in range(py, height, 2) for x in range(px, WIDTH, 2)]
        for core in range(2)
        for py in range(2)
        for px in range(2)
    ]


def first_kernel(order_ref, features_ref, blocked_ref, order_held, features_held, sems):
    order_move = pltpu.make_async_copy(order_ref, order_held, sems.at[0])
    features_move = pltpu.make_async_copy(features_ref, features_held, sems.at[1])
    order_move.start()
    features_move.start()
    order_move.wait()
    features_move.wait()
    blocked_ref[...] = matmul_tn(place_matrix(order_held), features_held[...]).astype(BF16)


def forward_kernel(rows_ref, cols_ref, tiles_ref, sources_ref, keep_ref, send_ref, total):
    core = lax.axis_index("row") & 1
    total[...] = jnp.zeros_like(total)
    for k in range(tiles_ref.shape[1]):
        side, kind, place = seat(rows_ref[0, k])
        product = matmul(tiles_ref[0, k], sources_ref[cols_ref[0, k]])
        total[side ^ core, kind, place] += product
    keep_ref[...] = total[0]
    send_ref[...] = total[1].astype(BF16)


def middle_kernel(
    parts_ref,
    blocked_ref,
    order_ref,
    w_self_ref,
    w_neigh_ref,
    bias_ref,
    cotangent_ref,
    hidden_ref,
    spread_ref,
    self_grad_ref,
):
    place = place_matrix(order_ref)
    aggregated = jnp.sum(parts_ref[...].astype(F32), axis=0).astype(BF16)
    pre_activation = (
        matmul(blocked_ref[...], w_self_ref[...])
        + matmul(aggregated, w_neigh_ref[...])
        + bias_ref[...]
    )
    squash = jax.nn.sigmoid(pre_activation)
    hidden_rows = (pre_activation * squash).astype(BF16)
    hidden_ref[...] = matmul(place, hidden_rows).astype(BF16)
    grad_rows = matmul_tn(place, cotangent_ref[...])
    grad_pre = (grad_rows * squash * (1.0 + pre_activation * (1.0 - squash))).astype(BF16)
    grad_agg = matmul_nt(w_neigh_ref[...], grad_pre).astype(BF16)
    spread_ref[...] = jnp.broadcast_to(grad_agg[None], spread_ref.shape)
    self_grad_ref[...] = matmul_nt(w_self_ref[...], grad_pre)


def backward_kernel(rows_ref, cols_ref, tiles_ref, near_ref, far_ref, parts_ref, total):
    core = lax.axis_index("row") & 1
    total[...] = jnp.zeros_like(total)
    for k in range(tiles_ref.shape[1]):
        side, kind, place = seat(rows_ref[0, k])
        grads = jnp.where(side == core, near_ref[kind, place], far_ref[kind, place])
        source = cols_ref[0, k]
        total[source & 1, source >> 1] += matmul(grads, tiles_ref[0, k])
    parts_ref[...] = total[...].astype(BF16)


def last_kernel(parts_ref, self_grad_ref, order_ref, out_ref):
    place = place_matrix(order_ref)
    grads = self_grad_ref[...] + jnp.sum(parts_ref[...].astype(F32), axis=0)
    high = grads.astype(BF16)
    rest = grads - high.astype(F32)
    middle = rest.astype(BF16)
    low = (rest - middle.astype(F32)).astype(BF16)
    out_ref[...] = matmul_nt(place, high) + (matmul_nt(place, middle) + matmul_nt(place, low))


def call(kernel, outs, specs, scratch=(), flops=0, limit=4):
    moved = sum(o.size * o.dtype.itemsize for o in outs)
    return pl.pallas_call(
        kernel,
        out_shape=outs,
        in_specs=specs,
        out_specs=[VMEM] * len(outs),
        scratch_shapes=list(scratch),
        compiler_params=pltpu.CompilerParams(vmem_limit_bytes=limit * 1024 * 1024),
        cost_estimate=pl.CostEstimate(flops=flops, bytes_accessed=moved, transcendentals=0),
    )


def per_device(
    features, node_order, adj_tiles, tile_rows, tile_cols, w_self, w_neigh, bias_vector, cotangent
):
    block, feat = features.shape
    hidden = w_self.shape[1]
    row_count = lax.axis_size("row")
    col_count = lax.axis_size("col")
    tiles = adj_tiles.shape[1]
    chips = row_count // 2
    places = chips // 4
    partners = [(i, i ^ 1) for i in range(row_count)]
    shape = jax.ShapeDtypeStruct
    tile_flops = 2 * tiles * block * block * feat

    (blocked,) = call(
        first_kernel,
        [shape((block, feat), BF16)],
        [ANY] * 2,
        [
            pltpu.VMEM(node_order.shape, node_order.dtype),
            pltpu.VMEM((block, feat), BF16),
            pltpu.SemaphoreType.DMA((2,)),
        ],
        limit=56,
    )(node_order, features)
    sources = lax.all_gather(blocked, "col", axis=0)
    keep, send = call(
        forward_kernel,
        [shape((4, places, block, feat), F32), shape((4, places, block, feat), BF16)],
        [SMEM, SMEM, VMEM, VMEM],
        [pltpu.VMEM((2, 4, places, block, feat), F32)],
        tile_flops,
        12,
    )(tile_rows, tile_cols, adj_tiles, sources)
    other = lax.ppermute(send, "row", partners)
    chip_sum = (keep + other.astype(F32)).astype(BF16)
    square = lax.all_to_all(chip_sum, "row", 0, 0, axis_index_groups=near_groups(chips, (1,)))
    class_sum = jnp.sum(square.astype(F32), axis=0).astype(BF16)
    parts = lax.all_to_all(class_sum, "row", 0, 0, axis_index_groups=far_groups(chips))
    hidden_out, spread, self_grad = call(
        middle_kernel,
        [
            shape((block, hidden), BF16),
            shape((places, feat, block), BF16),
            shape((feat, block), F32),
        ],
        [VMEM] * 7,
        limit=8,
    )(parts, blocked, node_order, w_self, w_neigh, bias_vector.reshape(1, hidden), cotangent)
    class_grads = lax.all_to_all(spread, "row", 0, 0, axis_index_groups=far_groups(chips))
    class_grads = jnp.broadcast_to(class_grads[None], (4,) + class_grads.shape)
    near = lax.all_to_all(class_grads, "row", 0, 0, axis_index_groups=near_groups(chips, ()))
    far = lax.ppermute(near, "row", partners)
    (source_parts,) = call(
        backward_kernel,
        [shape((2, col_count // 2, feat, block), BF16)],
        [SMEM, SMEM, VMEM, VMEM, VMEM],
        [pltpu.VMEM((2, col_count // 2, feat, block), F32)],
        tile_flops,
        8,
    )(tile_rows, tile_cols, adj_tiles, near, far)
    both = ("row", "col")
    pair = lax.all_to_all(
        source_parts, both, 0, 0, axis_index_groups=column_pairs(row_count, col_count, (1,))
    )
    pair_sum = (pair[0].astype(F32) + pair[1].astype(F32)).astype(BF16)
    own_parts = lax.all_to_all(
        pair_sum, both, 0, 0, axis_index_groups=column_halves(row_count, col_count)
    )
    (feature_grad,) = call(last_kernel, [shape((block, feat), F32)], [VMEM] * 3)(
        own_parts, self_grad, node_order
    )
    return (hidden_out, feature_grad)


def solution(mesh):
    placed = (
        P(("row", "col"), None),
        P(("row", "col"), None),
        P(("row", "col"), None, None, None),
        P(("row", "col"), None),
        P(("row", "col"), None),
        P(),
        P(),
        P(),
        P(("row", "col"), None),
    )
    return jax.shard_map(
        per_device,
        mesh=mesh,
        in_specs=placed,
        out_specs=(P(("row", "col"), None), P(("row", "col"), None)),
        check_vma=False,
    )
```

```python
import jax
import jax.numpy as jnp
from jax import lax
from jax.experimental import pallas as pl
from jax.experimental.pallas import tpu as pltpu
from jax.sharding import PartitionSpec as P

BF16 = jnp.bfloat16
F32 = jnp.float32
WIDTH = 4
VMEM = pl.BlockSpec(memory_space=pltpu.VMEM)
SMEM = pl.BlockSpec(memory_space=pltpu.SMEM)


def matmul(a, b):
    return lax.dot_general(a, b, (((1,), (0,)), ((), ())), preferred_element_type=F32)


def matmul_nt(a, b):
    return lax.dot_general(a, b, (((1,), (1,)), ((), ())), preferred_element_type=F32)


def matmul_tn(a, b):
    return lax.dot_general(a, b, (((0,), (0,)), ((), ())), preferred_element_type=F32)


def place_matrix(order_ref):
    order = order_ref[...]
    size = order.shape[1]
    nodes = lax.broadcasted_iota(jnp.int32, (size, size), 0)
    return jnp.where(nodes == order, 1.0, 0.0).astype(BF16)


def seat(target):
    core = target & 1
    kind = ((target >> 3) & 1) * 2 + ((target >> 1) & 1)
    place = (target >> 4) * 2 + ((target >> 2) & 1)
    return core, kind, place


def near_groups(chips):
    height = chips // WIDTH
    groups = []
    for core in range(2):
        for y in range(core, height + core, 2):
            for x in range(core, WIDTH + core, 2):
                ys = sorted([y % height, (y + 1) % height], key=lambda v: v % 2)
                xs = sorted([x % WIDTH, (x + 1) % WIDTH], key=lambda v: v % 2)
                groups.append([(b * WIDTH + a) * 2 + core for b in ys for a in xs])
    return groups


def far_groups(chips):
    height = chips // WIDTH
    return [
        [(y * WIDTH + x) * 2 + core for y in range(py, height, 2) for x in range(px, WIDTH, 2)]
        for core in range(2)
        for py in range(2)
        for px in range(2)
    ]


def order_kernel(order_ref, features_ref, blocked_ref):
    blocked_ref[0] = matmul_tn(place_matrix(order_ref), features_ref[...]).astype(BF16)


def forward_kernel(rows_ref, cols_ref, tiles_ref, sources_ref, keep_ref, send_ref, total):
    core = lax.axis_index("row") & 1
    total[...] = jnp.zeros_like(total)
    for k in range(tiles_ref.shape[1]):
        side, kind, place = seat(rows_ref[0, k])
        product = matmul(tiles_ref[0, k], sources_ref[cols_ref[0, k]])
        total[side ^ core, kind, place] += product
    keep_ref[...] = total[0]
    send_ref[...] = total[1].astype(BF16)


def middle_kernel(
    parts_ref,
    blocked_ref,
    order_ref,
    w_self_ref,
    w_neigh_ref,
    bias_ref,
    cotangent_ref,
    hidden_ref,
    spread_ref,
    self_grad_ref,
):
    place = place_matrix(order_ref)
    aggregated = jnp.sum(parts_ref[...].astype(F32), axis=0).astype(BF16)
    pre_activation = (
        matmul(blocked_ref[0], w_self_ref[...])
        + matmul(aggregated, w_neigh_ref[...])
        + bias_ref[...]
    )
    squash = jax.nn.sigmoid(pre_activation)
    hidden_rows = (pre_activation * squash).astype(BF16)
    hidden_ref[...] = matmul(place, hidden_rows).astype(BF16)
    grad_rows = matmul_tn(place, cotangent_ref[...])
    grad_pre = (grad_rows * squash * (1.0 + pre_activation * (1.0 - squash))).astype(BF16)
    grad_agg = matmul_nt(w_neigh_ref[...], grad_pre).astype(BF16)
    spread_ref[...] = jnp.broadcast_to(grad_agg[None], spread_ref.shape)
    self_grad_ref[...] = matmul_nt(w_self_ref[...], grad_pre)


def backward_kernel(rows_ref, cols_ref, tiles_ref, near_ref, far_ref, parts_ref, total):
    core = lax.axis_index("row") & 1
    total[...] = jnp.zeros_like(total)
    for k in range(tiles_ref.shape[1]):
        side, kind, place = seat(rows_ref[0, k])
        grads = jnp.where(side == core, near_ref[kind, place], far_ref[kind, place])
        total[cols_ref[0, k]] += matmul(grads, tiles_ref[0, k])
    parts_ref[...] = total[...].astype(BF16)


def last_kernel(parts_ref, self_grad_ref, order_ref, out_ref):
    place = place_matrix(order_ref)
    grads = self_grad_ref[...] + jnp.sum(parts_ref[...].astype(F32), axis=0)
    high = grads.astype(BF16)
    rest = grads - high.astype(F32)
    middle = rest.astype(BF16)
    low = (rest - middle.astype(F32)).astype(BF16)
    out_ref[...] = matmul_nt(place, high) + (matmul_nt(place, middle) + matmul_nt(place, low))


def call(kernel, outs, specs, scratch=(), flops=0, limit=4):
    moved = sum(o.size * o.dtype.itemsize for o in outs)
    return pl.pallas_call(
        kernel,
        out_shape=outs,
        in_specs=specs,
        out_specs=[VMEM] * len(outs),
        scratch_shapes=list(scratch),
        compiler_params=pltpu.CompilerParams(vmem_limit_bytes=limit * 1024 * 1024),
        cost_estimate=pl.CostEstimate(flops=flops, bytes_accessed=moved, transcendentals=0),
    )


def per_device(
    features, node_order, adj_tiles, tile_rows, tile_cols, w_self, w_neigh, bias_vector, cotangent
):
    block, feat = features.shape
    hidden = w_self.shape[1]
    row_count = lax.axis_size("row")
    col_count = lax.axis_size("col")
    tiles = adj_tiles.shape[1]
    chips = row_count // 2
    places = chips // 4
    partners = [(i, i ^ 1) for i in range(row_count)]
    shape = jax.ShapeDtypeStruct
    tile_flops = 2 * tiles * block * block * feat

    (blocked,) = call(
        order_kernel, [shape((1, block, feat), BF16)], [VMEM] * 2, flops=tile_flops * 16
    )(node_order, features)
    sources = lax.all_gather(blocked, "col", axis=0, tiled=True)
    keep, send = call(
        forward_kernel,
        [shape((4, places, block, feat), F32), shape((4, places, block, feat), BF16)],
        [SMEM, SMEM, VMEM, VMEM],
        [pltpu.VMEM((2, 4, places, block, feat), F32)],
        tile_flops,
        12,
    )(tile_rows, tile_cols, adj_tiles, sources)
    other = lax.ppermute(send, "row", partners)
    chip_sum = (keep + other.astype(F32)).astype(BF16)
    square = lax.all_to_all(chip_sum, "row", 0, 0, axis_index_groups=near_groups(chips))
    class_sum = jnp.sum(square.astype(F32), axis=0).astype(BF16)
    parts = lax.all_to_all(class_sum, "row", 0, 0, axis_index_groups=far_groups(chips))
    hidden_out, spread, self_grad = call(
        middle_kernel,
        [
            shape((block, hidden), BF16),
            shape((places, feat, block), BF16),
            shape((feat, block), F32),
        ],
        [VMEM] * 7,
        limit=8,
    )(parts, blocked, node_order, w_self, w_neigh, bias_vector.reshape(1, hidden), cotangent)
    class_grads = lax.all_to_all(spread, "row", 0, 0, axis_index_groups=far_groups(chips))
    class_grads = jnp.broadcast_to(class_grads[None], (4,) + class_grads.shape)
    near = lax.all_to_all(class_grads, "row", 0, 0, axis_index_groups=near_groups(chips))
    far = lax.ppermute(near, "row", partners)
    (source_parts,) = call(
        backward_kernel,
        [shape((col_count, feat, block), BF16)],
        [SMEM, SMEM, VMEM, VMEM, VMEM],
        [pltpu.VMEM((col_count, feat, block), F32)],
        tile_flops,
        8,
    )(tile_rows, tile_cols, adj_tiles, near, far)
    own_parts = lax.all_to_all(source_parts, "col", 0, 0)
    (feature_grad,) = call(last_kernel, [shape((block, feat), F32)], [VMEM] * 3)(
        own_parts, self_grad, node_order
    )
    return (hidden_out, feature_grad)


def solution(mesh):
    placed = (
        P(("row", "col"), None),
        P(("row", "col"), None),
        P(("row", "col"), None, None, None),
        P(("row", "col"), None),
        P(("row", "col"), None),
        P(),
        P(),
        P(),
        P(("row", "col"), None),
    )
    return jax.shard_map(
        per_device,
        mesh=mesh,
        in_specs=placed,
        out_specs=(P(("row", "col"), None), P(("row", "col"), None)),
        check_vma=False,
    )
```

```python
import jax
import jax.numpy as jnp
from jax import lax
from jax.experimental import pallas as pl
from jax.experimental.pallas import tpu as pltpu
from jax.sharding import PartitionSpec as P

BF16 = jnp.bfloat16
F32 = jnp.float32
WIDTH = 4
VMEM = pl.BlockSpec(memory_space=pltpu.VMEM)
SMEM = pl.BlockSpec(memory_space=pltpu.SMEM)


def matmul(a, b):
    return lax.dot_general(a, b, (((1,), (0,)), ((), ())), preferred_element_type=F32)


def matmul_nt(a, b):
    return lax.dot_general(a, b, (((1,), (1,)), ((), ())), preferred_element_type=F32)


def matmul_tn(a, b):
    return lax.dot_general(a, b, (((0,), (0,)), ((), ())), preferred_element_type=F32)


def seat(target):
    kind = ((target >> 3) & 1) * 2 + ((target >> 1) & 1)
    place = (target >> 4) * 2 + ((target >> 2) & 1)
    return target & 1, kind, place


def near_groups(chips):
    height = chips // WIDTH
    groups = []
    for core in range(2):
        for y in range(core, height + core, 2):
            for x in range(core, WIDTH + core, 2):
                ys = sorted([y % height, (y + 1) % height], key=lambda v: v % 2)
                xs = sorted([x % WIDTH, (x + 1) % WIDTH], key=lambda v: v % 2)
                groups.append([(b * WIDTH + a) * 2 + core for b in ys for a in xs])
    return groups


def far_groups(chips):
    height = chips // WIDTH
    return [
        [(y * WIDTH + x) * 2 + core for y in range(py, height, 2) for x in range(px, WIDTH, 2)]
        for core in range(2)
        for py in range(2)
        for px in range(2)
    ]


def node_kernel(nodes_ref):
    nodes_ref[...] = lax.broadcasted_iota(jnp.int32, nodes_ref.shape, 0)


def order_kernel(nodes_ref, order_ref, features_ref, place_ref, spread_ref):
    place = jnp.where(nodes_ref[...] == order_ref[...], 1.0, 0.0).astype(BF16)
    place_ref[...] = place
    blocked = matmul_tn(place, features_ref[...]).astype(BF16)
    spread_ref[...] = jnp.broadcast_to(blocked[None], spread_ref.shape)


def forward_kernel(rows_ref, cols_ref, tiles_ref, sources_ref, total_ref, send_ref):
    core = lax.axis_index("row") & 1
    total_ref[...] = jnp.zeros_like(total_ref)
    for k in range(tiles_ref.shape[1]):
        side, kind, place = seat(rows_ref[0, k])
        product = matmul(tiles_ref[0, k], sources_ref[cols_ref[0, k]])
        total_ref[side ^ core, kind, place] += product
    send_ref[...] = total_ref[1].astype(BF16)


def own_kernel(place_ref, blocked_ref, w_self_ref, bias_ref, cotangent_ref, own_ref, grad_rows_ref):
    own_ref[...] = matmul(blocked_ref[0], w_self_ref[...]) + bias_ref[...]
    grad_rows_ref[...] = matmul_tn(place_ref[...], cotangent_ref[...])


def middle_kernel(
    parts_ref, own_ref, grad_rows_ref, w_neigh_ref, hidden_ref, grad_pre_ref, spread_ref
):
    aggregated = jnp.sum(parts_ref[...].astype(F32), axis=0).astype(BF16)
    pre_activation = own_ref[...] + matmul(aggregated, w_neigh_ref[...])
    squash = jax.nn.sigmoid(pre_activation)
    hidden_ref[...] = (pre_activation * squash).astype(BF16)
    grad_pre = (grad_rows_ref[...] * squash * (1.0 + pre_activation * (1.0 - squash))).astype(BF16)
    grad_pre_ref[...] = grad_pre
    grad_agg = matmul_nt(w_neigh_ref[...], grad_pre).astype(BF16)
    spread_ref[...] = jnp.broadcast_to(grad_agg[None], spread_ref.shape)


def side_kernel(place_ref, hidden_ref, grad_pre_ref, w_self_ref, hidden_out_ref, self_grad_ref):
    hidden_out_ref[...] = matmul(place_ref[...], hidden_ref[...]).astype(BF16)
    self_grad_ref[...] = matmul_nt(w_self_ref[...], grad_pre_ref[...])


def backward_kernel(rows_ref, cols_ref, tiles_ref, near_ref, far_ref, parts_ref, total):
    core = lax.axis_index("row") & 1
    total[...] = jnp.zeros_like(total)
    for k in range(tiles_ref.shape[1]):
        side, kind, place = seat(rows_ref[0, k])
        grads = jnp.where(side == core, near_ref[kind, place], far_ref[kind, place])
        total[cols_ref[0, k]] += matmul(grads, tiles_ref[0, k])
    parts_ref[...] = total[...].astype(BF16)


def last_kernel(parts_ref, self_grad_ref, place_ref, out_ref):
    place = place_ref[...]
    grads = self_grad_ref[...] + jnp.sum(parts_ref[...].astype(F32), axis=0)
    high = grads.astype(BF16)
    rest = grads - high.astype(F32)
    middle = rest.astype(BF16)
    low = (rest - middle.astype(F32)).astype(BF16)
    out_ref[...] = matmul_nt(place, high) + (matmul_nt(place, middle) + matmul_nt(place, low))


def call(kernel, outs, specs, scratch=(), flops=0, limit=4):
    moved = sum(o.size * o.dtype.itemsize for o in outs)
    return pl.pallas_call(
        kernel,
        out_shape=outs,
        in_specs=specs,
        out_specs=[VMEM] * len(outs),
        scratch_shapes=list(scratch),
        compiler_params=pltpu.CompilerParams(vmem_limit_bytes=limit * 1024 * 1024),
        cost_estimate=pl.CostEstimate(flops=flops, bytes_accessed=moved, transcendentals=0),
    )


def per_device(
    features, node_order, adj_tiles, tile_rows, tile_cols, w_self, w_neigh, bias_vector, cotangent
):
    block, feat = features.shape
    hidden = w_self.shape[1]
    row_count = lax.axis_size("row")
    col_count = lax.axis_size("col")
    tiles = adj_tiles.shape[1]
    chips = row_count // 2
    places = chips // 4
    partners = [(i, i ^ 1) for i in range(row_count)]
    shape = jax.ShapeDtypeStruct
    tile_flops = 2 * tiles * block * block * feat

    (nodes,) = call(
        node_kernel, [shape((block, block), jnp.int32)], [], flops=tile_flops * 16
    )()
    place, own_spread = call(
        order_kernel, [shape((block, block), BF16), shape((col_count, block, feat), BF16)], [VMEM] * 3
    )(nodes, node_order, features)
    sources = lax.all_to_all(own_spread, "col", 0, 0)
    total, send = call(
        forward_kernel,
        [shape((2, 4, places, block, feat), F32), shape((4, places, block, feat), BF16)],
        [SMEM, SMEM, VMEM, VMEM],
        flops=tile_flops,
        limit=12,
    )(tile_rows, tile_cols, adj_tiles, sources)
    other = lax.ppermute(send, "row", partners)
    total, own_spread = lax.optimization_barrier((total, own_spread))
    own, grad_rows = call(
        own_kernel,
        [shape((block, hidden), F32), shape((block, hidden), F32)],
        [VMEM] * 5,
        flops=tile_flops,
    )(place, own_spread[:1], w_self, bias_vector.reshape(1, hidden), cotangent)
    other, own, grad_rows = lax.optimization_barrier((other, own, grad_rows))
    chip_sum = (total[0] + other.astype(F32)).astype(BF16)
    square = lax.all_to_all(chip_sum, "row", 0, 0, axis_index_groups=near_groups(chips))
    class_sum = jnp.sum(square.astype(F32), axis=0).astype(BF16)
    parts = lax.all_to_all(class_sum, "row", 0, 0, axis_index_groups=far_groups(chips))
    hidden_rows, grad_pre, spread = call(
        middle_kernel,
        [
            shape((block, hidden), BF16),
            shape((block, hidden), BF16),
            shape((places, feat, block), BF16),
        ],
        [VMEM] * 4,
        limit=8,
    )(parts, own, grad_rows, w_neigh)
    class_grads = lax.all_to_all(
        spread, "row", 0, 0, axis_index_groups=far_groups(chips)
    )
    class_grads = jnp.broadcast_to(class_grads[None], (4,) + class_grads.shape)
    near = lax.all_to_all(
        class_grads, "row", 0, 0, axis_index_groups=near_groups(chips)
    )
    near, hidden_rows, grad_pre = lax.optimization_barrier((near, hidden_rows, grad_pre))
    far = lax.ppermute(near, "row", partners)
    hidden_out, self_grad = call(
        side_kernel,
        [shape((block, hidden), BF16), shape((feat, block), F32)],
        [VMEM] * 4,
        flops=tile_flops,
    )(place, hidden_rows, grad_pre, w_self)
    far, hidden_out, self_grad = lax.optimization_barrier((far, hidden_out, self_grad))
    (source_parts,) = call(
        backward_kernel,
        [shape((col_count, feat, block), BF16)],
        [SMEM, SMEM, VMEM, VMEM, VMEM],
        [pltpu.VMEM((col_count, feat, block), F32)],
        tile_flops,
        8,
    )(tile_rows, tile_cols, adj_tiles, near, far)
    own_parts = lax.all_to_all(source_parts, "col", 0, 0)
    (feature_grad,) = call(last_kernel, [shape((block, feat), F32)], [VMEM] * 3)(
        own_parts, self_grad, place
    )
    return (hidden_out, feature_grad)


def solution(mesh):
    placed = (
        P(("row", "col"), None),
        P(("row", "col"), None),
        P(("row", "col"), None, None, None),
        P(("row", "col"), None),
        P(("row", "col"), None),
        P(),
        P(),
        P(),
        P(("row", "col"), None),
    )
    return jax.shard_map(
        per_device,
        mesh=mesh,
        in_specs=placed,
        out_specs=(P(("row", "col"), None), P(("row", "col"), None)),
        check_vma=False,
    )
```

```python
import jax
import jax.numpy as jnp
from jax import lax
from jax.experimental import pallas as pl
from jax.experimental.pallas import tpu as pltpu
from jax.sharding import PartitionSpec as P

BF16 = jnp.bfloat16
F32 = jnp.float32
WIDTH = 4
VMEM = pl.BlockSpec(memory_space=pltpu.VMEM)
SMEM = pl.BlockSpec(memory_space=pltpu.SMEM)


def matmul(a, b):
    return lax.dot_general(a, b, (((1,), (0,)), ((), ())), preferred_element_type=F32)


def matmul_nt(a, b):
    return lax.dot_general(a, b, (((1,), (1,)), ((), ())), preferred_element_type=F32)


def matmul_tn(a, b):
    return lax.dot_general(a, b, (((0,), (0,)), ((), ())), preferred_element_type=F32)


def seat(target):
    kind = ((target >> 3) & 1) * 2 + ((target >> 1) & 1)
    place = (target >> 4) * 2 + ((target >> 2) & 1)
    return target & 1, kind, place


def near_groups(chips):
    height = chips // WIDTH
    groups = []
    for core in range(2):
        for y in range(core, height + core, 2):
            for x in range(core, WIDTH + core, 2):
                ys = sorted([y % height, (y + 1) % height], key=lambda v: v % 2)
                xs = sorted([x % WIDTH, (x + 1) % WIDTH], key=lambda v: v % 2)
                groups.append([(b * WIDTH + a) * 2 + core for b in ys for a in xs])
    return groups


def far_groups(chips):
    height = chips // WIDTH
    return [
        [(y * WIDTH + x) * 2 + core for y in range(py, height, 2) for x in range(px, WIDTH, 2)]
        for core in range(2)
        for py in range(2)
        for px in range(2)
    ]


def node_kernel(nodes_ref):
    nodes_ref[...] = lax.broadcasted_iota(jnp.int32, nodes_ref.shape, 0)


def order_kernel(nodes_ref, order_ref, features_ref, place_ref, blocked_ref):
    place = jnp.where(nodes_ref[...] == order_ref[...], 1.0, 0.0).astype(BF16)
    place_ref[...] = place
    blocked_ref[0] = matmul_tn(place, features_ref[...]).astype(BF16)


def forward_kernel(rows_ref, cols_ref, tiles_ref, sources_ref, total_ref, send_ref):
    core = lax.axis_index("row") & 1
    total_ref[...] = jnp.zeros_like(total_ref)
    for k in range(tiles_ref.shape[1]):
        side, kind, place = seat(rows_ref[0, k])
        product = matmul(tiles_ref[0, k], sources_ref[cols_ref[0, k]])
        total_ref[side ^ core, kind, place] += product
    send_ref[...] = total_ref[1].astype(BF16)


def own_kernel(place_ref, blocked_ref, w_self_ref, bias_ref, cotangent_ref, own_ref, grad_rows_ref):
    own_ref[...] = matmul(blocked_ref[0], w_self_ref[...]) + bias_ref[...]
    grad_rows_ref[...] = matmul_tn(place_ref[...], cotangent_ref[...])


def middle_kernel(
    parts_ref, own_ref, grad_rows_ref, w_neigh_ref, hidden_ref, grad_pre_ref, spread_ref
):
    aggregated = jnp.sum(parts_ref[...].astype(F32), axis=0).astype(BF16)
    pre_activation = own_ref[...] + matmul(aggregated, w_neigh_ref[...])
    squash = jax.nn.sigmoid(pre_activation)
    hidden_ref[...] = (pre_activation * squash).astype(BF16)
    grad_pre = (grad_rows_ref[...] * squash * (1.0 + pre_activation * (1.0 - squash))).astype(BF16)
    grad_pre_ref[...] = grad_pre
    grad_agg = matmul_nt(w_neigh_ref[...], grad_pre).astype(BF16)
    spread_ref[...] = jnp.broadcast_to(grad_agg[None], spread_ref.shape)


def side_kernel(place_ref, hidden_ref, grad_pre_ref, w_self_ref, hidden_out_ref, self_grad_ref):
    hidden_out_ref[...] = matmul(place_ref[...], hidden_ref[...]).astype(BF16)
    self_grad_ref[...] = matmul_nt(w_self_ref[...], grad_pre_ref[...])


def backward_kernel(rows_ref, cols_ref, tiles_ref, near_ref, far_ref, parts_ref, total):
    core = lax.axis_index("row") & 1
    total[...] = jnp.zeros_like(total)
    for k in range(tiles_ref.shape[1]):
        side, kind, place = seat(rows_ref[0, k])
        grads = jnp.where(side == core, near_ref[kind, place], far_ref[kind, place])
        total[cols_ref[0, k]] += matmul(grads, tiles_ref[0, k])
    parts_ref[...] = total[...].astype(BF16)


def last_kernel(parts_ref, self_grad_ref, place_ref, out_ref):
    place = place_ref[...]
    grads = self_grad_ref[...] + jnp.sum(parts_ref[...].astype(F32), axis=0)
    high = grads.astype(BF16)
    rest = grads - high.astype(F32)
    middle = rest.astype(BF16)
    low = (rest - middle.astype(F32)).astype(BF16)
    out_ref[...] = matmul_nt(place, high) + (matmul_nt(place, middle) + matmul_nt(place, low))


def call(kernel, outs, specs, scratch=(), flops=0, limit=4):
    moved = sum(o.size * o.dtype.itemsize for o in outs)
    return pl.pallas_call(
        kernel,
        out_shape=outs,
        in_specs=specs,
        out_specs=[VMEM] * len(outs),
        scratch_shapes=list(scratch),
        compiler_params=pltpu.CompilerParams(vmem_limit_bytes=limit * 1024 * 1024),
        cost_estimate=pl.CostEstimate(flops=flops, bytes_accessed=moved, transcendentals=0),
    )


def per_device(
    features, node_order, adj_tiles, tile_rows, tile_cols, w_self, w_neigh, bias_vector, cotangent
):
    block, feat = features.shape
    hidden = w_self.shape[1]
    row_count = lax.axis_size("row")
    col_count = lax.axis_size("col")
    tiles = adj_tiles.shape[1]
    chips = row_count // 2
    places = chips // 4
    partners = [(i, i ^ 1) for i in range(row_count)]
    shape = jax.ShapeDtypeStruct
    tile_flops = 2 * tiles * block * block * feat

    (nodes,) = call(
        node_kernel, [shape((block, block), jnp.int32)], [], flops=tile_flops * 16
    )()
    place, blocked = call(
        order_kernel, [shape((block, block), BF16), shape((1, block, feat), BF16)], [VMEM] * 3
    )(nodes, node_order, features)
    sources = lax.all_gather(blocked, "col", axis=0, tiled=True)
    total, send = call(
        forward_kernel,
        [shape((2, 4, places, block, feat), F32), shape((4, places, block, feat), BF16)],
        [SMEM, SMEM, VMEM, VMEM],
        flops=tile_flops,
        limit=12,
    )(tile_rows, tile_cols, adj_tiles, sources)
    other = lax.ppermute(send, "row", partners)
    total, blocked = lax.optimization_barrier((total, blocked))
    own, grad_rows = call(
        own_kernel,
        [shape((block, hidden), F32), shape((block, hidden), F32)],
        [VMEM] * 5,
        flops=tile_flops,
    )(place, blocked, w_self, bias_vector.reshape(1, hidden), cotangent)
    other, own, grad_rows = lax.optimization_barrier((other, own, grad_rows))
    chip_sum = (total[0] + other.astype(F32)).astype(BF16)
    square = lax.all_to_all(chip_sum, "row", 0, 0, axis_index_groups=near_groups(chips))
    class_sum = jnp.sum(square.astype(F32), axis=0).astype(BF16)
    parts = lax.all_to_all(class_sum, "row", 0, 0, axis_index_groups=far_groups(chips))
    hidden_rows, grad_pre, spread = call(
        middle_kernel,
        [
            shape((block, hidden), BF16),
            shape((block, hidden), BF16),
            shape((places, feat, block), BF16),
        ],
        [VMEM] * 4,
        limit=8,
    )(parts, own, grad_rows, w_neigh)
    class_grads = lax.all_to_all(spread, "row", 0, 0, axis_index_groups=far_groups(chips))
    class_grads = jnp.broadcast_to(class_grads[None], (4,) + class_grads.shape)
    near = lax.all_to_all(class_grads, "row", 0, 0, axis_index_groups=near_groups(chips))
    near, hidden_rows, grad_pre = lax.optimization_barrier((near, hidden_rows, grad_pre))
    far = lax.ppermute(near, "row", partners)
    hidden_out, self_grad = call(
        side_kernel,
        [shape((block, hidden), BF16), shape((feat, block), F32)],
        [VMEM] * 4,
        flops=tile_flops,
    )(place, hidden_rows, grad_pre, w_self)
    far, hidden_out, self_grad = lax.optimization_barrier((far, hidden_out, self_grad))
    (source_parts,) = call(
        backward_kernel,
        [shape((col_count, feat, block), BF16)],
        [SMEM, SMEM, VMEM, VMEM, VMEM],
        [pltpu.VMEM((col_count, feat, block), F32)],
        tile_flops,
        8,
    )(tile_rows, tile_cols, adj_tiles, near, far)
    own_parts = lax.all_to_all(source_parts, "col", 0, 0)
    (feature_grad,) = call(last_kernel, [shape((block, feat), F32)], [VMEM] * 3)(
        own_parts, self_grad, place
    )
    return (hidden_out, feature_grad)


def solution(mesh):
    placed = (
        P(("row", "col"), None),
        P(("row", "col"), None),
        P(("row", "col"), None, None, None),
        P(("row", "col"), None),
        P(("row", "col"), None),
        P(),
        P(),
        P(),
        P(("row", "col"), None),
    )
    return jax.shard_map(
        per_device,
        mesh=mesh,
        in_specs=placed,
        out_specs=(P(("row", "col"), None), P(("row", "col"), None)),
        check_vma=False,
    )
```

```python
import jax
import jax.numpy as jnp
from jax import lax
from jax.experimental import pallas as pl
from jax.experimental.pallas import tpu as pltpu
from jax.sharding import PartitionSpec as P

BF16 = jnp.bfloat16
F32 = jnp.float32
WIDTH = 4
VMEM = pl.BlockSpec(memory_space=pltpu.VMEM)
SMEM = pl.BlockSpec(memory_space=pltpu.SMEM)


def matmul(a, b):
    return lax.dot_general(a, b, (((1,), (0,)), ((), ())), preferred_element_type=F32)


def matmul_nt(a, b):
    return lax.dot_general(a, b, (((1,), (1,)), ((), ())), preferred_element_type=F32)


def matmul_tn(a, b):
    return lax.dot_general(a, b, (((0,), (0,)), ((), ())), preferred_element_type=F32)


def seat(target):
    kind = ((target >> 3) & 1) * 2 + ((target >> 1) & 1)
    place = (target >> 4) * 2 + ((target >> 2) & 1)
    return target & 1, kind, place


def near_groups(chips):
    height = chips // WIDTH
    groups = []
    for core in range(2):
        for y in range(core, height + core, 2):
            for x in range(core, WIDTH + core, 2):
                ys = sorted([y % height, (y + 1) % height], key=lambda v: v % 2)
                xs = sorted([x % WIDTH, (x + 1) % WIDTH], key=lambda v: v % 2)
                groups.append([(b * WIDTH + a) * 2 + core for b in ys for a in xs])
    return groups


def far_groups(chips):
    height = chips // WIDTH
    return [
        [(y * WIDTH + x) * 2 + core for y in range(py, height, 2) for x in range(px, WIDTH, 2)]
        for core in range(2)
        for py in range(2)
        for px in range(2)
    ]


def column_pairs(rows, cols):
    return [
        [row * cols + c for c in sorted([col % cols, (col + 1) % cols], key=lambda v: v % 2)]
        for row in range(rows)
        for col in range(row % 2, cols + row % 2, 2)
    ]


def column_halves(rows, cols):
    return [
        [row * cols + c for c in range(odd, cols, 2)] for row in range(rows) for odd in range(2)
    ]


def node_kernel(nodes_ref):
    nodes_ref[...] = lax.broadcasted_iota(jnp.int32, nodes_ref.shape, 0)


def order_kernel(nodes_ref, order_ref, features_ref, place_ref, blocked_ref, spread_ref):
    place = jnp.where(nodes_ref[...] == order_ref[...], 1.0, 0.0).astype(BF16)
    place_ref[...] = place
    blocked = matmul_tn(place, features_ref[...]).astype(BF16)
    blocked_ref[0] = blocked
    spread_ref[...] = jnp.broadcast_to(blocked[None], spread_ref.shape)


def forward_kernel(rows_ref, cols_ref, tiles_ref, sources_ref, total_ref, send_ref):
    core = lax.axis_index("row") & 1
    total_ref[...] = jnp.zeros_like(total_ref)
    for k in range(tiles_ref.shape[1]):
        side, kind, place = seat(rows_ref[0, k])
        source = cols_ref[0, k]
        product = matmul(tiles_ref[0, k], sources_ref[source & 1, source >> 1])
        total_ref[side ^ core, kind, place] += product
    send_ref[...] = total_ref[1].astype(BF16)


def own_kernel(place_ref, blocked_ref, w_self_ref, bias_ref, cotangent_ref, own_ref, grad_rows_ref):
    own_ref[...] = matmul(blocked_ref[0], w_self_ref[...]) + bias_ref[...]
    grad_rows_ref[...] = matmul_tn(place_ref[...], cotangent_ref[...])


def middle_kernel(
    parts_ref, own_ref, grad_rows_ref, w_neigh_ref, hidden_ref, grad_pre_ref, spread_ref
):
    aggregated = jnp.sum(parts_ref[...].astype(F32), axis=0).astype(BF16)
    pre_activation = own_ref[...] + matmul(aggregated, w_neigh_ref[...])
    squash = jax.nn.sigmoid(pre_activation)
    hidden_ref[...] = (pre_activation * squash).astype(BF16)
    grad_pre = (grad_rows_ref[...] * squash * (1.0 + pre_activation * (1.0 - squash))).astype(BF16)
    grad_pre_ref[...] = grad_pre
    grad_agg = matmul_nt(w_neigh_ref[...], grad_pre).astype(BF16)
    spread_ref[...] = jnp.broadcast_to(grad_agg[None], spread_ref.shape)


def side_kernel(place_ref, hidden_ref, grad_pre_ref, w_self_ref, hidden_out_ref, self_grad_ref):
    hidden_out_ref[...] = matmul(place_ref[...], hidden_ref[...]).astype(BF16)
    self_grad_ref[...] = matmul_nt(w_self_ref[...], grad_pre_ref[...])


def backward_kernel(rows_ref, cols_ref, tiles_ref, near_ref, far_ref, parts_ref, total):
    core = lax.axis_index("row") & 1
    total[...] = jnp.zeros_like(total)
    for k in range(tiles_ref.shape[1]):
        side, kind, place = seat(rows_ref[0, k])
        grads = jnp.where(side == core, near_ref[kind, place], far_ref[kind, place])
        total[cols_ref[0, k]] += matmul(grads, tiles_ref[0, k])
    parts_ref[...] = total[...].astype(BF16)


def last_kernel(parts_ref, self_grad_ref, place_ref, out_ref):
    place = place_ref[...]
    grads = self_grad_ref[...] + jnp.sum(parts_ref[...].astype(F32), axis=0)
    high = grads.astype(BF16)
    rest = grads - high.astype(F32)
    middle = rest.astype(BF16)
    low = (rest - middle.astype(F32)).astype(BF16)
    out_ref[...] = matmul_nt(place, high) + (matmul_nt(place, middle) + matmul_nt(place, low))


def call(kernel, outs, specs, scratch=(), flops=0, limit=4):
    moved = sum(o.size * o.dtype.itemsize for o in outs)
    return pl.pallas_call(
        kernel,
        out_shape=outs,
        in_specs=specs,
        out_specs=[VMEM] * len(outs),
        scratch_shapes=list(scratch),
        compiler_params=pltpu.CompilerParams(vmem_limit_bytes=limit * 1024 * 1024),
        cost_estimate=pl.CostEstimate(flops=flops, bytes_accessed=moved, transcendentals=0),
    )


def per_device(
    features, node_order, adj_tiles, tile_rows, tile_cols, w_self, w_neigh, bias_vector, cotangent
):
    block, feat = features.shape
    hidden = w_self.shape[1]
    row_count = lax.axis_size("row")
    col_count = lax.axis_size("col")
    tiles = adj_tiles.shape[1]
    chips = row_count // 2
    places = chips // 4
    partners = [(i, i ^ 1) for i in range(row_count)]
    shape = jax.ShapeDtypeStruct
    tile_flops = 2 * tiles * block * block * feat

    (nodes,) = call(
        node_kernel, [shape((block, block), jnp.int32)], [], flops=tile_flops * 16
    )()
    place, blocked, spread = call(
        order_kernel,
        [
            shape((block, block), BF16),
            shape((1, block, feat), BF16),
            shape((col_count // 2, block, feat), BF16),
        ],
        [VMEM] * 3,
    )(nodes, node_order, features)
    both = ("row", "col")
    half = lax.all_to_all(
        spread, both, 0, 0, axis_index_groups=column_halves(row_count, col_count)
    )
    half = jnp.broadcast_to(half[None], (2,) + half.shape)
    sources = lax.all_to_all(
        half, both, 0, 0, axis_index_groups=column_pairs(row_count, col_count)
    )
    total, send = call(
        forward_kernel,
        [shape((2, 4, places, block, feat), F32), shape((4, places, block, feat), BF16)],
        [SMEM, SMEM, VMEM, VMEM],
        flops=tile_flops,
        limit=12,
    )(tile_rows, tile_cols, adj_tiles, sources)
    other = lax.ppermute(send, "row", partners)
    total, blocked = lax.optimization_barrier((total, blocked))
    own, grad_rows = call(
        own_kernel,
        [shape((block, hidden), F32), shape((block, hidden), F32)],
        [VMEM] * 5,
        flops=tile_flops,
    )(place, blocked, w_self, bias_vector.reshape(1, hidden), cotangent)
    other, own, grad_rows = lax.optimization_barrier((other, own, grad_rows))
    chip_sum = (total[0] + other.astype(F32)).astype(BF16)
    square = lax.all_to_all(chip_sum, "row", 0, 0, axis_index_groups=near_groups(chips))
    class_sum = jnp.sum(square.astype(F32), axis=0).astype(BF16)
    parts = lax.all_to_all(class_sum, "row", 0, 0, axis_index_groups=far_groups(chips))
    hidden_rows, grad_pre, spread = call(
        middle_kernel,
        [
            shape((block, hidden), BF16),
            shape((block, hidden), BF16),
            shape((places, feat, block), BF16),
        ],
        [VMEM] * 4,
        limit=8,
    )(parts, own, grad_rows, w_neigh)
    class_grads = lax.all_to_all(spread, "row", 0, 0, axis_index_groups=far_groups(chips))
    class_grads = jnp.broadcast_to(class_grads[None], (4,) + class_grads.shape)
    near = lax.all_to_all(class_grads, "row", 0, 0, axis_index_groups=near_groups(chips))
    near, hidden_rows, grad_pre = lax.optimization_barrier((near, hidden_rows, grad_pre))
    far = lax.ppermute(near, "row", partners)
    hidden_out, self_grad = call(
        side_kernel,
        [shape((block, hidden), BF16), shape((feat, block), F32)],
        [VMEM] * 4,
        flops=tile_flops,
    )(place, hidden_rows, grad_pre, w_self)
    far, hidden_out, self_grad = lax.optimization_barrier((far, hidden_out, self_grad))
    (source_parts,) = call(
        backward_kernel,
        [shape((col_count, feat, block), BF16)],
        [SMEM, SMEM, VMEM, VMEM, VMEM],
        [pltpu.VMEM((col_count, feat, block), F32)],
        tile_flops,
        8,
    )(tile_rows, tile_cols, adj_tiles, near, far)
    own_parts = lax.all_to_all(source_parts, "col", 0, 0)
    (feature_grad,) = call(last_kernel, [shape((block, feat), F32)], [VMEM] * 3)(
        own_parts, self_grad, place
    )
    return (hidden_out, feature_grad)


def solution(mesh):
    placed = (
        P(("row", "col"), None),
        P(("row", "col"), None),
        P(("row", "col"), None, None, None),
        P(("row", "col"), None),
        P(("row", "col"), None),
        P(),
        P(),
        P(),
        P(("row", "col"), None),
    )
    return jax.shard_map(
        per_device,
        mesh=mesh,
        in_specs=placed,
        out_specs=(P(("row", "col"), None), P(("row", "col"), None)),
        check_vma=False,
    )
```

```python
import jax
import jax.numpy as jnp
from jax import lax
from jax.experimental import pallas as pl
from jax.experimental.pallas import tpu as pltpu
from jax.sharding import PartitionSpec as P

BF16 = jnp.bfloat16
F32 = jnp.float32
WIDTH = 4
VMEM = pl.BlockSpec(memory_space=pltpu.VMEM)
SMEM = pl.BlockSpec(memory_space=pltpu.SMEM)


def matmul(a, b):
    return lax.dot_general(a, b, (((1,), (0,)), ((), ())), preferred_element_type=F32)


def matmul_nt(a, b):
    return lax.dot_general(a, b, (((1,), (1,)), ((), ())), preferred_element_type=F32)


def matmul_tn(a, b):
    return lax.dot_general(a, b, (((0,), (0,)), ((), ())), preferred_element_type=F32)


def seat(target):
    kind = ((target >> 3) & 1) * 2 + ((target >> 1) & 1)
    place = (target >> 4) * 2 + ((target >> 2) & 1)
    return target & 1, kind, place


def near_groups(chips):
    height = chips // WIDTH
    groups = []
    for core in range(2):
        for y in range(core, height + core, 2):
            for x in range(core, WIDTH + core, 2):
                ys = sorted([y % height, (y + 1) % height], key=lambda v: v % 2)
                xs = sorted([x % WIDTH, (x + 1) % WIDTH], key=lambda v: v % 2)
                groups.append([(b * WIDTH + a) * 2 + core for b in ys for a in xs])
    return groups


def far_groups(chips):
    height = chips // WIDTH
    return [
        [(y * WIDTH + x) * 2 + core for y in range(py, height, 2) for x in range(px, WIDTH, 2)]
        for core in range(2)
        for py in range(2)
        for px in range(2)
    ]


def column_pairs(rows, cols):
    return [[row * cols + c, row * cols + c + 1] for row in range(rows) for c in range(0, cols, 2)]


def column_halves(rows, cols):
    return [
        [row * cols + c for c in range(odd, cols, 2)] for row in range(rows) for odd in range(2)
    ]


def node_kernel(nodes_ref):
    nodes_ref[...] = lax.broadcasted_iota(jnp.int32, nodes_ref.shape, 0)


def order_kernel(nodes_ref, order_ref, features_ref, place_ref, blocked_ref):
    place = jnp.where(nodes_ref[...] == order_ref[...], 1.0, 0.0).astype(BF16)
    place_ref[...] = place
    blocked_ref[0] = matmul_tn(place, features_ref[...]).astype(BF16)


def forward_kernel(rows_ref, cols_ref, tiles_ref, sources_ref, total_ref, send_ref):
    core = lax.axis_index("row") & 1
    total_ref[...] = jnp.zeros_like(total_ref)
    for k in range(tiles_ref.shape[1]):
        side, kind, place = seat(rows_ref[0, k])
        product = matmul(tiles_ref[0, k], sources_ref[cols_ref[0, k]])
        total_ref[side ^ core, kind, place] += product
    send_ref[...] = total_ref[1].astype(BF16)


def own_kernel(place_ref, blocked_ref, w_self_ref, bias_ref, cotangent_ref, own_ref, grad_rows_ref):
    own_ref[...] = matmul(blocked_ref[0], w_self_ref[...]) + bias_ref[...]
    grad_rows_ref[...] = matmul_tn(place_ref[...], cotangent_ref[...])


def middle_kernel(
    parts_ref, own_ref, grad_rows_ref, w_neigh_ref, hidden_ref, grad_pre_ref, spread_ref
):
    aggregated = jnp.sum(parts_ref[...].astype(F32), axis=0).astype(BF16)
    pre_activation = own_ref[...] + matmul(aggregated, w_neigh_ref[...])
    squash = jax.nn.sigmoid(pre_activation)
    hidden_ref[...] = (pre_activation * squash).astype(BF16)
    grad_pre = (grad_rows_ref[...] * squash * (1.0 + pre_activation * (1.0 - squash))).astype(BF16)
    grad_pre_ref[...] = grad_pre
    grad_agg = matmul_nt(w_neigh_ref[...], grad_pre).astype(BF16)
    spread_ref[...] = jnp.broadcast_to(grad_agg[None], spread_ref.shape)


def side_kernel(place_ref, hidden_ref, grad_pre_ref, w_self_ref, hidden_out_ref, self_grad_ref):
    hidden_out_ref[...] = matmul(place_ref[...], hidden_ref[...]).astype(BF16)
    self_grad_ref[...] = matmul_nt(w_self_ref[...], grad_pre_ref[...])


def backward_kernel(rows_ref, cols_ref, tiles_ref, near_ref, far_ref, parts_ref, total):
    core = lax.axis_index("row") & 1
    half = total.shape[0] // 2
    total[...] = jnp.zeros_like(total)
    for k in range(tiles_ref.shape[1]):
        side, kind, place = seat(rows_ref[0, k])
        grads = jnp.where(side == core, near_ref[kind, place], far_ref[kind, place])
        source = cols_ref[0, k]
        halved = (source & 1) * half + (source >> 1)
        total[jnp.where(core == 0, source, halved)] += matmul(grads, tiles_ref[0, k])
    parts_ref[...] = total[...].astype(BF16)


def last_kernel(parts_ref, self_grad_ref, place_ref, out_ref):
    place = place_ref[...]
    grads = self_grad_ref[...] + jnp.sum(parts_ref[...].astype(F32), axis=0)
    high = grads.astype(BF16)
    rest = grads - high.astype(F32)
    middle = rest.astype(BF16)
    low = (rest - middle.astype(F32)).astype(BF16)
    out_ref[...] = matmul_nt(place, high) + (matmul_nt(place, middle) + matmul_nt(place, low))


def call(kernel, outs, specs, scratch=(), flops=0, limit=4):
    moved = sum(o.size * o.dtype.itemsize for o in outs)
    return pl.pallas_call(
        kernel,
        out_shape=outs,
        in_specs=specs,
        out_specs=[VMEM] * len(outs),
        scratch_shapes=list(scratch),
        compiler_params=pltpu.CompilerParams(vmem_limit_bytes=limit * 1024 * 1024),
        cost_estimate=pl.CostEstimate(flops=flops, bytes_accessed=moved, transcendentals=0),
    )


def per_device(
    features, node_order, adj_tiles, tile_rows, tile_cols, w_self, w_neigh, bias_vector, cotangent
):
    block, feat = features.shape
    hidden = w_self.shape[1]
    row_count = lax.axis_size("row")
    col_count = lax.axis_size("col")
    tiles = adj_tiles.shape[1]
    chips = row_count // 2
    places = chips // 4
    partners = [(i, i ^ 1) for i in range(row_count)]
    shape = jax.ShapeDtypeStruct
    tile_flops = 2 * tiles * block * block * feat

    (nodes,) = call(
        node_kernel, [shape((block, block), jnp.int32)], [], flops=tile_flops * 16
    )()
    place, blocked = call(
        order_kernel, [shape((block, block), BF16), shape((1, block, feat), BF16)], [VMEM] * 3
    )(nodes, node_order, features)
    even_core = (lax.axis_index("row") & 1) == 0
    sources = lax.cond(
        even_core,
        lambda own: lax.all_to_all(
            jnp.broadcast_to(own, (col_count, block, feat)), "col", 0, 0
        ),
        lambda own: lax.all_gather(own, "col", axis=0, tiled=True),
        blocked,
    )
    total, send = call(
        forward_kernel,
        [shape((2, 4, places, block, feat), F32), shape((4, places, block, feat), BF16)],
        [SMEM, SMEM, VMEM, VMEM],
        flops=tile_flops,
        limit=12,
    )(tile_rows, tile_cols, adj_tiles, sources)
    other = lax.ppermute(send, "row", partners)
    total, blocked = lax.optimization_barrier((total, blocked))
    own, grad_rows = call(
        own_kernel,
        [shape((block, hidden), F32), shape((block, hidden), F32)],
        [VMEM] * 5,
        flops=tile_flops,
    )(place, blocked, w_self, bias_vector.reshape(1, hidden), cotangent)
    other, own, grad_rows = lax.optimization_barrier((other, own, grad_rows))
    chip_sum = (total[0] + other.astype(F32)).astype(BF16)
    square = lax.all_to_all(chip_sum, "row", 0, 0, axis_index_groups=near_groups(chips))
    class_sum = jnp.sum(square.astype(F32), axis=0).astype(BF16)
    parts = lax.all_to_all(class_sum, "row", 0, 0, axis_index_groups=far_groups(chips))
    hidden_rows, grad_pre, spread = call(
        middle_kernel,
        [
            shape((block, hidden), BF16),
            shape((block, hidden), BF16),
            shape((places, feat, block), BF16),
        ],
        [VMEM] * 4,
        limit=8,
    )(parts, own, grad_rows, w_neigh)
    class_grads = lax.all_to_all(spread, "row", 0, 0, axis_index_groups=far_groups(chips))
    class_grads = jnp.broadcast_to(class_grads[None], (4,) + class_grads.shape)
    near = lax.all_to_all(class_grads, "row", 0, 0, axis_index_groups=near_groups(chips))
    near, hidden_rows, grad_pre = lax.optimization_barrier((near, hidden_rows, grad_pre))
    far = lax.ppermute(near, "row", partners)
    hidden_out, self_grad = call(
        side_kernel,
        [shape((block, hidden), BF16), shape((feat, block), F32)],
        [VMEM] * 4,
        flops=tile_flops,
    )(place, hidden_rows, grad_pre, w_self)
    far, hidden_out, self_grad = lax.optimization_barrier((far, hidden_out, self_grad))
    (source_parts,) = call(
        backward_kernel,
        [shape((col_count, feat, block), BF16)],
        [SMEM, SMEM, VMEM, VMEM, VMEM],
        [pltpu.VMEM((col_count, feat, block), F32)],
        tile_flops,
        8,
    )(tile_rows, tile_cols, adj_tiles, near, far)
    def finish(parts, self_grad, place):
        return call(last_kernel, [shape((block, feat), F32)], [VMEM] * 3)(parts, self_grad, place)[0]

    def direct(parts, self_grad, place):
        return finish(lax.all_to_all(parts, "col", 0, 0), self_grad, place)

    def staged(parts, self_grad, place):
        both = ("row", "col")
        pairs = column_pairs(row_count, col_count)
        halves = column_halves(row_count, col_count)
        pair = lax.all_to_all(
            parts.reshape(2, col_count // 2, feat, block), both, 0, 0, axis_index_groups=pairs
        )
        pair_sum = (pair[0].astype(F32) + pair[1].astype(F32)).astype(BF16)
        return finish(
            lax.all_to_all(pair_sum, both, 0, 0, axis_index_groups=halves), self_grad, place
        )

    feature_grad = lax.cond(even_core, direct, staged, source_parts, self_grad, place)
    return (hidden_out, feature_grad)


def solution(mesh):
    placed = (
        P(("row", "col"), None),
        P(("row", "col"), None),
        P(("row", "col"), None, None, None),
        P(("row", "col"), None),
        P(("row", "col"), None),
        P(),
        P(),
        P(),
        P(("row", "col"), None),
    )
    return jax.shard_map(
        per_device,
        mesh=mesh,
        in_specs=placed,
        out_specs=(P(("row", "col"), None), P(("row", "col"), None)),
        check_vma=False,
    )
```

```python
import jax
import jax.numpy as jnp
from jax import lax
from jax.experimental import pallas as pl
from jax.experimental.pallas import tpu as pltpu
from jax.sharding import PartitionSpec as P

BF16 = jnp.bfloat16
F32 = jnp.float32
WIDTH = 4
VMEM = pl.BlockSpec(memory_space=pltpu.VMEM)
SMEM = pl.BlockSpec(memory_space=pltpu.SMEM)


def matmul(a, b):
    return lax.dot_general(a, b, (((1,), (0,)), ((), ())), preferred_element_type=F32)


def matmul_nt(a, b):
    return lax.dot_general(a, b, (((1,), (1,)), ((), ())), preferred_element_type=F32)


def matmul_tn(a, b):
    return lax.dot_general(a, b, (((0,), (0,)), ((), ())), preferred_element_type=F32)


def seat(target):
    kind = ((target >> 3) & 1) * 2 + ((target >> 1) & 1)
    place = (target >> 4) * 2 + ((target >> 2) & 1)
    return target & 1, kind, place


def near_groups(chips):
    height = chips // WIDTH
    groups = []
    for core in range(2):
        for y in range(core, height + core, 2):
            for x in range(core, WIDTH + core, 2):
                ys = sorted([y % height, (y + 1) % height], key=lambda v: v % 2)
                xs = sorted([x % WIDTH, (x + 1) % WIDTH], key=lambda v: v % 2)
                groups.append([(b * WIDTH + a) * 2 + core for b in ys for a in xs])
    return groups


def far_groups(chips):
    height = chips // WIDTH
    return [
        [(y * WIDTH + x) * 2 + core for y in range(py, height, 2) for x in range(px, WIDTH, 2)]
        for core in range(2)
        for py in range(2)
        for px in range(2)
    ]


def column_pairs(rows, cols):
    return [[row * cols + c, row * cols + c + 1] for row in range(rows) for c in range(0, cols, 2)]


def column_halves(rows, cols):
    return [
        [row * cols + c for c in range(odd, cols, 2)] for row in range(rows) for odd in range(2)
    ]


def node_kernel(nodes_ref):
    nodes_ref[...] = lax.broadcasted_iota(jnp.int32, nodes_ref.shape, 0)


def order_kernel(nodes_ref, order_ref, features_ref, place_ref, blocked_ref):
    place = jnp.where(nodes_ref[...] == order_ref[...], 1.0, 0.0).astype(BF16)
    place_ref[...] = place
    blocked_ref[0] = matmul_tn(place, features_ref[...]).astype(BF16)


def forward_kernel(rows_ref, cols_ref, tiles_ref, sources_ref, total_ref, send_ref):
    core = lax.axis_index("row") & 1
    half = sources_ref.shape[0] // 2
    total_ref[...] = jnp.zeros_like(total_ref)
    for k in range(tiles_ref.shape[1]):
        side, kind, place = seat(rows_ref[0, k])
        source = cols_ref[0, k]
        halved = (source & 1) * half + (source >> 1)
        product = matmul(tiles_ref[0, k], sources_ref[jnp.where(core == 0, source, halved)])
        total_ref[side ^ core, kind, place] += product
    send_ref[...] = total_ref[1].astype(BF16)


def own_kernel(place_ref, blocked_ref, w_self_ref, bias_ref, cotangent_ref, own_ref, grad_rows_ref):
    own_ref[...] = matmul(blocked_ref[0], w_self_ref[...]) + bias_ref[...]
    grad_rows_ref[...] = matmul_tn(place_ref[...], cotangent_ref[...])


def middle_kernel(
    parts_ref, own_ref, grad_rows_ref, w_neigh_ref, hidden_ref, grad_pre_ref, spread_ref
):
    aggregated = jnp.sum(parts_ref[...].astype(F32), axis=0).astype(BF16)
    pre_activation = own_ref[...] + matmul(aggregated, w_neigh_ref[...])
    squash = jax.nn.sigmoid(pre_activation)
    hidden_ref[...] = (pre_activation * squash).astype(BF16)
    grad_pre = (grad_rows_ref[...] * squash * (1.0 + pre_activation * (1.0 - squash))).astype(BF16)
    grad_pre_ref[...] = grad_pre
    grad_agg = matmul_nt(w_neigh_ref[...], grad_pre).astype(BF16)
    spread_ref[...] = jnp.broadcast_to(grad_agg[None], spread_ref.shape)


def side_kernel(place_ref, hidden_ref, grad_pre_ref, w_self_ref, hidden_out_ref, self_grad_ref):
    hidden_out_ref[...] = matmul(place_ref[...], hidden_ref[...]).astype(BF16)
    self_grad_ref[...] = matmul_nt(w_self_ref[...], grad_pre_ref[...])


def backward_kernel(rows_ref, cols_ref, tiles_ref, near_ref, far_ref, parts_ref, total):
    core = lax.axis_index("row") & 1
    half = total.shape[0] // 2
    total[...] = jnp.zeros_like(total)
    for k in range(tiles_ref.shape[1]):
        side, kind, place = seat(rows_ref[0, k])
        grads = jnp.where(side == core, near_ref[kind, place], far_ref[kind, place])
        source = cols_ref[0, k]
        halved = (source & 1) * half + (source >> 1)
        total[jnp.where(core == 0, source, halved)] += matmul(grads, tiles_ref[0, k])
    parts_ref[...] = total[...].astype(BF16)


def last_kernel(parts_ref, self_grad_ref, place_ref, out_ref):
    place = place_ref[...]
    grads = self_grad_ref[...] + jnp.sum(parts_ref[...].astype(F32), axis=0)
    high = grads.astype(BF16)
    rest = grads - high.astype(F32)
    middle = rest.astype(BF16)
    low = (rest - middle.astype(F32)).astype(BF16)
    out_ref[...] = matmul_nt(place, high) + (matmul_nt(place, middle) + matmul_nt(place, low))


def call(kernel, outs, specs, scratch=(), flops=0, limit=4):
    moved = sum(o.size * o.dtype.itemsize for o in outs)
    return pl.pallas_call(
        kernel,
        out_shape=outs,
        in_specs=specs,
        out_specs=[VMEM] * len(outs),
        scratch_shapes=list(scratch),
        compiler_params=pltpu.CompilerParams(vmem_limit_bytes=limit * 1024 * 1024),
        cost_estimate=pl.CostEstimate(flops=flops, bytes_accessed=moved, transcendentals=0),
    )


def per_device(
    features, node_order, adj_tiles, tile_rows, tile_cols, w_self, w_neigh, bias_vector, cotangent
):
    block, feat = features.shape
    hidden = w_self.shape[1]
    row_count = lax.axis_size("row")
    col_count = lax.axis_size("col")
    tiles = adj_tiles.shape[1]
    chips = row_count // 2
    places = chips // 4
    partners = [(i, i ^ 1) for i in range(row_count)]
    shape = jax.ShapeDtypeStruct
    tile_flops = 2 * tiles * block * block * feat

    (nodes,) = call(
        node_kernel, [shape((block, block), jnp.int32)], [], flops=tile_flops * 16
    )()
    place, blocked = call(
        order_kernel, [shape((block, block), BF16), shape((1, block, feat), BF16)], [VMEM] * 3
    )(nodes, node_order, features)
    even_core = (lax.axis_index("row") & 1) == 0

    def staged_gather(own):
        both = ("row", "col")
        half = col_count // 2
        own = jnp.broadcast_to(own, (half, block, feat))
        own = lax.all_to_all(
            own, both, 0, 0, axis_index_groups=column_halves(row_count, col_count)
        )
        own = jnp.broadcast_to(own[None], (2, half, block, feat))
        own = lax.all_to_all(own, both, 0, 0, axis_index_groups=column_pairs(row_count, col_count))
        return own.reshape(col_count, block, feat)

    sources = lax.cond(
        even_core,
        lambda own: lax.all_to_all(
            jnp.broadcast_to(own, (col_count, block, feat)), "col", 0, 0
        ),
        staged_gather,
        blocked,
    )
    total, send = call(
        forward_kernel,
        [shape((2, 4, places, block, feat), F32), shape((4, places, block, feat), BF16)],
        [SMEM, SMEM, VMEM, VMEM],
        flops=tile_flops,
        limit=12,
    )(tile_rows, tile_cols, adj_tiles, sources)
    other = lax.ppermute(send, "row", partners)
    total, blocked = lax.optimization_barrier((total, blocked))
    own, grad_rows = call(
        own_kernel,
        [shape((block, hidden), F32), shape((block, hidden), F32)],
        [VMEM] * 5,
        flops=tile_flops,
    )(place, blocked, w_self, bias_vector.reshape(1, hidden), cotangent)
    other, own, grad_rows = lax.optimization_barrier((other, own, grad_rows))
    chip_sum = (total[0] + other.astype(F32)).astype(BF16)
    square = lax.all_to_all(chip_sum, "row", 0, 0, axis_index_groups=near_groups(chips))
    class_sum = jnp.sum(square.astype(F32), axis=0).astype(BF16)
    parts = lax.all_to_all(class_sum, "row", 0, 0, axis_index_groups=far_groups(chips))
    hidden_rows, grad_pre, spread = call(
        middle_kernel,
        [
            shape((block, hidden), BF16),
            shape((block, hidden), BF16),
            shape((places, feat, block), BF16),
        ],
        [VMEM] * 4,
        limit=8,
    )(parts, own, grad_rows, w_neigh)
    class_grads = lax.all_to_all(spread, "row", 0, 0, axis_index_groups=far_groups(chips))
    class_grads = jnp.broadcast_to(class_grads[None], (4,) + class_grads.shape)
    near = lax.all_to_all(class_grads, "row", 0, 0, axis_index_groups=near_groups(chips))
    near, hidden_rows, grad_pre = lax.optimization_barrier((near, hidden_rows, grad_pre))
    far = lax.ppermute(near, "row", partners)
    hidden_out, self_grad = call(
        side_kernel,
        [shape((block, hidden), BF16), shape((feat, block), F32)],
        [VMEM] * 4,
        flops=tile_flops,
    )(place, hidden_rows, grad_pre, w_self)
    far, hidden_out, self_grad = lax.optimization_barrier((far, hidden_out, self_grad))
    (source_parts,) = call(
        backward_kernel,
        [shape((col_count, feat, block), BF16)],
        [SMEM, SMEM, VMEM, VMEM, VMEM],
        [pltpu.VMEM((col_count, feat, block), F32)],
        tile_flops,
        8,
    )(tile_rows, tile_cols, adj_tiles, near, far)
    def finish(parts, self_grad, place):
        return call(last_kernel, [shape((block, feat), F32)], [VMEM] * 3)(parts, self_grad, place)[0]

    def direct(parts, self_grad, place):
        return finish(lax.all_to_all(parts, "col", 0, 0), self_grad, place)

    def staged(parts, self_grad, place):
        both = ("row", "col")
        pairs = column_pairs(row_count, col_count)
        halves = column_halves(row_count, col_count)
        pair = lax.all_to_all(
            parts.reshape(2, col_count // 2, feat, block), both, 0, 0, axis_index_groups=pairs
        )
        pair_sum = (pair[0].astype(F32) + pair[1].astype(F32)).astype(BF16)
        return finish(
            lax.all_to_all(pair_sum, both, 0, 0, axis_index_groups=halves), self_grad, place
        )

    feature_grad = lax.cond(even_core, direct, staged, source_parts, self_grad, place)
    return (hidden_out, feature_grad)


def solution(mesh):
    placed = (
        P(("row", "col"), None),
        P(("row", "col"), None),
        P(("row", "col"), None, None, None),
        P(("row", "col"), None),
        P(("row", "col"), None),
        P(),
        P(),
        P(),
        P(("row", "col"), None),
    )
    return jax.shard_map(
        per_device,
        mesh=mesh,
        in_specs=placed,
        out_specs=(P(("row", "col"), None), P(("row", "col"), None)),
        check_vma=False,
    )
```
